256 devices in a mesh: seq: 64 (over z, y, core), head: 4 (over x).
Axes of the slice: x: 4, y: 4, z: 8, core: 2. Of those that a mesh axis runs over, the one named last changes fastest.
Arguments:
- queries: bfloat16 [6, 8, 128, 128], P(None, None, 'head'), may hold values from -16 to 16
- key_cache: bfloat16 [6, 122880, 8, 128], P(None, 'seq', 'head'), may hold values from -16 to 16
- value_cache: bfloat16 [6, 122880, 8, 128], P(None, 'seq', 'head'), may hold values from -12 to 12
- grad_out: bfloat16 [6, 8, 128, 128], P(None, None, 'head'), may hold values from -20 to 20
- cache_len: int32 [6], replicated, may hold values from 61440 to 122880, as said below
Outputs:
- grad_queries: bfloat16 [6, 8, 128, 128], P(None, None, 'head')
The draws below stay inside these ranges and needn't reach their ends.
Inputs may be any that keep to these rules, and one draw needn't show every extreme that they name: The 8 queries of sequence b stand at positions cache_len[b] - 8 to cache_len[b] - 1 of its cache. Some sequence has all 122880 positions valid.
All inputs are finite; a program needn't handle non-finite values.
Results may differ from the reference program's by a relative error of at most 0.0058.
Values may be sent and summed in bfloat16 or wider, within the bound.
No kernel may reach another device: no remote copies, remote signals or barrier semaphores. Data moves between devices by JAX's collectives and lax.ppermute only.
A program may use at most 128 MiB of HBM per device.

```python
import math
import jax
import jax.numpy as jnp
from jax import lax

B = 6
QT = 8
HQ = 128
KVH = 8
HD = 128
TOTAL = 122880


def draw_cache_len(key, part):
    key = jax.random.fold_in(key, 1)
    key_length, key_order = jax.random.split(key)
    lengths = jax.random.randint(key_length, (B,), TOTAL // 2, TOTAL + 1, dtype=jnp.int32)
    chosen = jax.random.randint(key_order, (), 0, B, dtype=jnp.int32)
    full = jnp.arange(B, dtype=jnp.int32) == chosen
    lengths = jnp.where(full, TOTAL, lengths)
    return lengths.astype(jnp.int32)


def draw_key_cache(key, part):
    key = jax.random.fold_in(key, 2)
    key_base, key_mean = jax.random.split(key, 2)
    centre = jax.random.normal(key_mean, (1, 1, KVH, HD), jnp.float32)
    cache_data = jax.random.normal(key_base, (B, TOTAL, KVH, HD), jnp.float32) + centre
    return jnp.clip(cache_data, -16.0, 16.0).astype(jnp.bfloat16)


def draw_value_cache(key, part):
    key = jax.random.fold_in(key, 3)
    key_base, key_mean = jax.random.split(key)
    centre = jax.random.normal(key_mean, (1, 1, KVH, HD), jnp.float32)
    cache_data = jax.random.normal(key_base, (B, TOTAL, KVH, HD), jnp.float32) + centre
    return jnp.clip(cache_data, -12.0, 12.0).astype(jnp.bfloat16)


def draw_queries(key, part):
    key = jax.random.fold_in(key, 4)
    query_data = jax.random.normal(key, (B, QT, HQ, HD), jnp.float32)
    return jnp.clip(query_data, -16.0, 16.0).astype(jnp.bfloat16)


def draw_grad_out(key, part):
    key = jax.random.fold_in(key, 5)
    ramp = jnp.exp(math.log(3.0) * jnp.arange(HQ, dtype=jnp.float32) / (HQ - 1))[None, None, :, None]
    grad_data = jax.random.normal(key, (B, QT, HQ, HD), jnp.float32) * ramp
    return jnp.clip(grad_data, -20.0, 20.0).astype(jnp.bfloat16)


def setup_inputs(seed: int = 0) -> dict:
    keys = jax.random.split(jax.random.key(seed), 6)
    queries = draw_queries(jax.random.fold_in(keys[5], 71), 0)
    key_cache = draw_key_cache(jax.random.fold_in(keys[5], 71), 0)
    value_cache = draw_value_cache(jax.random.fold_in(keys[5], 71), 0)
    grad_out = draw_grad_out(jax.random.fold_in(keys[5], 71), 0)
    cache_len = draw_cache_len(jax.random.fold_in(keys[5], 71), 0)
    return {"queries": queries, "key_cache": key_cache, "value_cache": value_cache, "grad_out": grad_out, "cache_len": cache_len}


NEGATIVE = -1e+30
EPSILON = 1e-06

def group_term(query_rows, grad_rows, keys_group, values_group, length):
    groups = HQ // KVH
    score_scale = 1.0 / math.sqrt(HD)
    scores = jnp.dot(query_rows, keys_group.T, preferred_element_type=jnp.float32) * score_scale
    row_token = jnp.arange(QT * groups, dtype=jnp.int32) // groups
    key_index = jnp.arange(TOTAL, dtype=jnp.int32)
    visible = key_index[None, :] <= (length - QT + row_token)[:, None]
    masked = jnp.where(visible, scores, NEGATIVE)
    row_max = lax.optimization_barrier(jnp.max(masked, axis=1, keepdims=True))
    weights = jnp.where(visible, jnp.exp(masked - row_max), 0.0)
    softmax_total = lax.optimization_barrier(jnp.sum(weights, axis=1, keepdims=True))
    grad_prob = jnp.dot(grad_rows, values_group.T, preferred_element_type=jnp.float32)
    out_dot = lax.optimization_barrier(jnp.sum(weights * grad_prob, axis=1, keepdims=True)) / softmax_total
    grad_score = (weights / softmax_total * (grad_prob - out_dot)).astype(jnp.bfloat16)
    return jnp.dot(grad_score, keys_group, preferred_element_type=jnp.float32) * score_scale

def reference(queries, key_cache, value_cache, grad_out, cache_len):
    groups = HQ // KVH

    def one_group(item_index):
        sequence = (item_index // KVH).astype(jnp.int32)
        kv_head = (item_index % KVH).astype(jnp.int32)
        anchor = jnp.zeros((), jnp.int32)
        head_start = (kv_head * groups).astype(jnp.int32)
        query_rows = lax.dynamic_slice(queries, (sequence, anchor, head_start, anchor), (1, QT, groups, HD)).reshape(QT * groups, HD)
        grad_rows = lax.dynamic_slice(grad_out, (sequence, anchor, head_start, anchor), (1, QT, groups, HD)).reshape(QT * groups, HD)
        keys_group = lax.dynamic_slice(key_cache, (sequence, anchor, kv_head, anchor), (1, TOTAL, 1, HD)).reshape(TOTAL, HD)
        values_group = lax.dynamic_slice(value_cache, (sequence, anchor, kv_head, anchor), (1, TOTAL, 1, HD)).reshape(TOTAL, HD)
        length = lax.dynamic_index_in_dim(cache_len, sequence, 0, keepdims=False).astype(jnp.int32)
        return group_term(query_rows, grad_rows, keys_group, values_group, length)
    pieces = lax.map(one_group, jnp.arange(B * KVH, dtype=jnp.int32))
    grad_sum = pieces.reshape(B, KVH, QT, groups, HD).transpose(0, 2, 1, 3, 4).reshape(B, QT, HQ, HD)
    norm_scale = jnp.sqrt(jnp.mean(grad_sum * grad_sum) + EPSILON)
    return (grad_sum / norm_scale).astype(jnp.bfloat16)
```

```python
import math

import jax
import jax.numpy as jnp
from jax import lax
from jax.experimental import pallas as pl
from jax.experimental.pallas import tpu as pltpu
from jax.sharding import Mesh
from jax.sharding import PartitionSpec as P

B = 6
QT = 8
HQ = 128
HD = 128

NEGATIVE = -1e30
FLOOR = -1e29
EPSILON = 1e-06
SCALE = 1.0 / math.sqrt(HD)
SCALE2 = SCALE * math.log2(math.e)
CHUNK = 256
TILES = CHUNK // 8
PARTS = 3
SLOT = 56
MIB = 1024 * 1024
VMEM = pl.BlockSpec(memory_space=pltpu.VMEM)
HBM = pl.BlockSpec(memory_space=pltpu.HBM)
FIRST = (((0,), (0,)), ((), ()))


def high(x):
    return x.astype(jnp.bfloat16).astype(jnp.float32)


def attend(
    len_ref, q_hbm, k_hbm, v_hbm, go_hbm, peer_ref, own_ref, own_st_ref,
    q_buf, go_buf, k_buf, v_buf, s_a, s_b, s_c, g_a, g_b, g_c, sems,
):
    core = lax.axis_index("c")
    count, rows = k_buf.shape[0], k_buf.shape[1]
    span = rows // 2
    chunks = rows // CHUNK
    start = ((lax.axis_index("z") * 4 + lax.axis_index("y")) * 2 + core) * span

    def sequence(j):
        return 2 * j + 1 - core if j < PARTS else 2 * (j - PARTS) + core

    small = [
        pltpu.make_async_copy(q_hbm, q_buf, sems.at[2 * count]),
        pltpu.make_async_copy(go_hbm, go_buf, sems.at[2 * count + 1]),
    ]
    keys = [pltpu.make_async_copy(k_hbm.at[sequence(j)], k_buf.at[j], sems.at[2 * j]) for j in range(count)]
    values = [pltpu.make_async_copy(v_hbm.at[sequence(j)], v_buf.at[j], sems.at[2 * j + 1]) for j in range(count)]
    small[0].start()
    keys[0].start()
    small[1].start()
    values[0].start()
    for j in range(1, count):
        keys[j].start()
        values[j].start()

    scores, probs = (s_a, s_b, s_c), (g_a, g_b, g_c)
    even8 = lax.broadcasted_iota(jnp.int32, (8, 128), 0) % 2 == 0
    odd_row = lax.broadcasted_iota(jnp.int32, (CHUNK, 128), 0) % 2 == 1
    keep_odd = odd_row.astype(jnp.float32).astype(jnp.bfloat16)
    keep_even = (1.0 - odd_row.astype(jnp.float32)).astype(jnp.bfloat16)
    lead = lax.broadcasted_iota(jnp.int32, (8, 128), 1) // 16 - lax.broadcasted_iota(jnp.int32, (8, 128), 0) // 2
    tile_start = lax.broadcasted_iota(jnp.int32, (TILES, 8, 128), 0) * 4

    def turned(x):
        both = jnp.concatenate([x[:, :16].reshape(128, HD), x[:, 16:].reshape(128, HD)], axis=0)
        return both.T

    def sides(x, reduce, fill):
        return (
            reduce(jnp.where(even8, x, fill), axis=0, keepdims=True),
            reduce(jnp.where(even8, fill, x), axis=0, keepdims=True),
        )

    def score_step(j, i, qt, gt, room, top):
        at = slice(i * CHUNK, (i + 1) * CHUNK)
        s = jnp.dot(k_buf[j, at, :], qt, preferred_element_type=jnp.float32)
        s = jnp.where(odd_row, s[:, 128:], s[:, :128]).reshape(TILES, 8, 128)
        s = jnp.where((room + lead - i * (CHUNK // 2))[None] >= tile_start, s, NEGATIVE)
        scores[j % 3][at, :] = s.reshape(CHUNK, 128)
        g = jnp.dot(v_buf[j, at, :], gt, preferred_element_type=jnp.float32)
        probs[j % 3][at, :] = jnp.where(odd_row, g[:, 128:], g[:, :128])
        return jnp.maximum(top, jnp.max(s, axis=0))

    def weight_step(j, i, tops, total, dot):
        at = slice(i * CHUNK, (i + 1) * CHUNK)
        s = scores[j % 3][at, :].reshape(TILES, 8, 128)
        w = jnp.exp2((s - tops[None]) * SCALE2)
        scores[j % 3][at, :] = w.reshape(CHUNK, 128)
        wg = w * probs[j % 3][at, :].reshape(TILES, 8, 128)
        return total + jnp.sum(w, axis=0), dot + jnp.sum(wg, axis=0)

    def term_step(j, i, dots, acc):
        at = slice(i * CHUNK, (i + 1) * CHUNK)
        w = scores[j % 3][at, :].reshape(TILES, 8, 128)
        p = w * (probs[j % 3][at, :].reshape(TILES, 8, 128) - dots[None])
        pw = jnp.concatenate([p.reshape(CHUNK, 128), w.reshape(CHUNK, 128)], axis=1).astype(jnp.bfloat16)
        kc = k_buf[j, at, :]
        kk = jnp.concatenate([kc * keep_even, kc * keep_odd], axis=1)
        return acc + lax.dot_general(pw, kk, FIRST, preferred_element_type=jnp.float32)

    def prepare(j):
        seq = sequence(j)
        keys[j].wait()
        values[j].wait()
        return turned(q_buf[seq]), turned(go_buf[seq]), len_ref[seq] - QT - start

    def reference_of(top):
        return [high(jnp.maximum(m, FLOOR)) for m in sides(top, jnp.max, NEGATIVE)]

    def means_of(total, dot):
        totals = sides(total, jnp.sum, 0.0)
        dots = [
            jnp.where(t > 0.0, d / jnp.where(t > 0.0, t, 1.0), 0.0)
            for t, d in zip(totals, sides(dot, jnp.sum, 0.0))
        ]
        return totals, dots

    def store(j, acc, tops, totals, dots):
        pieces = []
        for half in (acc[:128], acc[128:]):
            pair = [half[:, side * 128 : (side + 1) * 128].reshape(8, 16, 128) for side in range(2)]
            pieces.append(jnp.concatenate(pair, axis=1).reshape(32, 8, 128))
        both = jnp.concatenate(pieces, axis=1)
        part = j % PARTS
        if j < PARTS:
            peer_ref[:, part * 16 : part * 16 + 16, :] = both.astype(jnp.bfloat16)
        else:
            own_ref[:, part * 16 : part * 16 + 16, :] = both
        sub = lax.broadcasted_iota(jnp.int32, (8, 128), 0)
        for side in range(2):
            if j < PARTS:
                t, d = totals[side], dots[side]
                cols = (tops[side], high(t), t - high(t), high(d), d - high(d))
            else:
                cols = (tops[side], totals[side], dots[side])
            block = jnp.zeros((8, 128), jnp.float32)
            for k, col in enumerate(cols):
                block = jnp.where(sub == k, col, block)
            blocks[j // PARTS, side, part] = block

    blocks = {}
    for copy in small:
        copy.wait()
    zero8 = jnp.zeros((8, 128), jnp.float32)
    stats = {}
    for n in range(count + 2):
        first, second, third = n, n - 1, n - 2
        if first < count:
            ready = prepare(first)
            top = jnp.full((8, 128), NEGATIVE, jnp.float32)
        if 0 <= second < count:
            tops = reference_of(last_top)
            tops8 = jnp.where(even8, *tops)
            total, dot = zero8, zero8
        if 0 <= third:
            dots8 = jnp.where(even8, *stats[third][2])
            acc = jnp.zeros((256, 256), jnp.float32)
        for i in range(chunks):
            if 0 <= third:
                acc = term_step(third, i, dots8, acc)
            if first < count:
                top = score_step(first, i, *ready, top)
            if 0 <= second < count:
                total, dot = weight_step(second, i, tops8, total, dot)
        if 0 <= third:
            store(third, acc, *stats[third])
        if 0 <= second < count:
            stats[second] = (tops, *means_of(total, dot))
        last_top = top

    blank = jnp.zeros((8, 128), jnp.float32)
    z = jnp.concatenate(
        [blocks.get((who, side, part), blank) for who in range(2) for side in range(2) for part in range(4)], axis=0
    ).T
    for who in range(2):
        pair = []
        for side in range(2):
            shift = (128 - who * 64 - side * 32) % 128
            pair.append((pltpu.roll(z, shift, 1) if shift else z).reshape(8, 16, 128))
        st = jnp.concatenate(pair, axis=1).reshape(32, 8, 128)
        if who == 0:
            peer_ref[:, 48:64, :] = jnp.concatenate([st, jnp.zeros_like(st)], axis=1).astype(jnp.bfloat16)
        else:
            own_st_ref[...] = st


def attend_call(lengths, q, k, v, go):
    count, span = k.shape[0], k.shape[1]
    k = k.reshape(count, span * 2, HD)
    v = v.reshape(count, span * 2, HD)
    wide = pltpu.VMEM((span * 2, 128), jnp.float32)
    return pl.pallas_call(
        attend,
        in_specs=[pl.BlockSpec(memory_space=pltpu.SMEM), HBM, HBM, HBM, HBM],
        out_specs=[VMEM, VMEM, VMEM],
        out_shape=[
            jax.ShapeDtypeStruct((32, 64, HD), jnp.bfloat16),
            jax.ShapeDtypeStruct((32, 48, HD), jnp.float32),
            jax.ShapeDtypeStruct((32, 8, HD), jnp.float32),
        ],
        scratch_shapes=[
            pltpu.VMEM(q.shape, jnp.bfloat16),
            pltpu.VMEM(go.shape, jnp.bfloat16),
            pltpu.VMEM(k.shape, jnp.bfloat16),
            pltpu.VMEM(v.shape, jnp.bfloat16),
            wide, wide, wide, wide, wide, wide,
            pltpu.SemaphoreType.DMA((2 * count + 2,)),
        ],
        compiler_params=pltpu.CompilerParams(vmem_limit_bytes=60 * MIB),
        cost_estimate=pl.CostEstimate(flops=4_500_000_000, bytes_accessed=14_000_000, transcendentals=3_000_000),
    )(lengths, q, k, v, go)


def column(st, part, k):
    at = 8 * part + k
    return st[:, :, at : at + 1]


def pair_up(peer_ref, own_ref, own_st_ref, out_ref):
    peer = peer_ref[...].astype(jnp.float32)
    own = own_ref[...]
    peer_st, own_st = peer[:, 48:56], own_st_ref[...]
    lane = lax.broadcasted_iota(jnp.int32, (32, 8, 128), 2)
    st = jnp.zeros((32, 8, 128), jnp.float32)
    pieces = []
    for part in range(PARTS):
        at = part * 16
        top_a, total_a, dot_a = (column(own_st, part, k) for k in range(3))
        top_b = column(peer_st, part, 0)
        total_b = column(peer_st, part, 1) + column(peer_st, part, 2)
        dot_b = column(peer_st, part, 3) + column(peer_st, part, 4)
        top = jnp.maximum(top_a, top_b)
        factor_a = jnp.exp2((top_a - top) * SCALE2)
        factor_b = jnp.exp2((top_b - top) * SCALE2)
        total_a, total_b = factor_a * total_a, factor_b * total_b
        total = total_a + total_b
        dot = (total_a * dot_a + total_b * dot_b) / jnp.where(total > 0.0, total, 1.0)
        term_a, term_b = own[:, at : at + 8], peer[:, at : at + 8]
        mass_a, mass_b = own[:, at + 8 : at + 16], peer[:, at + 8 : at + 16]
        pieces.append(
            factor_a * term_a + (factor_a * (dot_a - dot)) * mass_a
            + (factor_b * term_b + (factor_b * (dot_b - dot)) * mass_b)
        )
        pieces.append(factor_a * mass_a + factor_b * mass_b)
        for k, col in enumerate((top, high(total), total - high(total), high(dot), dot - high(dot))):
            st = jnp.where(lane == 8 * part + k, col, st)
    out_ref[...] = jnp.concatenate(pieces + [st], axis=1).astype(jnp.bfloat16)


def pair_up_call(peer, own, own_st):
    return pl.pallas_call(
        pair_up,
        in_specs=[VMEM] * 3,
        out_specs=VMEM,
        out_shape=jax.ShapeDtypeStruct((32, SLOT, HD), jnp.bfloat16),
        compiler_params=pltpu.CompilerParams(vmem_limit_bytes=24 * MIB),
        cost_estimate=pl.CostEstimate(flops=4_000_000, bytes_accessed=2_000_000, transcendentals=1000),
    )(peer, own, own_st)


def merge(msg_ref, out_ref):
    msg = msg_ref[...].astype(jnp.float32)
    st = msg[:, 48:56]
    rows = []
    for part in range(PARTS):
        at = part * 16
        top = column(st, part, 0)
        total = column(st, part, 1) + column(st, part, 2)
        dot = column(st, part, 3) + column(st, part, 4)
        factor = jnp.exp2((top - jnp.max(top, axis=0, keepdims=True)) * SCALE2)
        total = factor * total
        whole = jnp.sum(total, axis=0, keepdims=True)
        mean = jnp.sum(total * dot, axis=0, keepdims=True) / whole
        grad = jnp.sum(factor * msg[:, at : at + 8] + (factor * (dot - mean)) * msg[:, at + 8 : at + 16], axis=0)
        rows.append(grad * (SCALE / whole[0]))
    block = jnp.concatenate(rows, axis=0).astype(jnp.bfloat16)
    out_ref[...] = jnp.broadcast_to(block[None], out_ref.shape)


def merge_call(msg):
    return pl.pallas_call(
        merge,
        in_specs=[VMEM],
        out_specs=VMEM,
        out_shape=jax.ShapeDtypeStruct((32, 8 * PARTS, HD), jnp.bfloat16),
        compiler_params=pltpu.CompilerParams(vmem_limit_bytes=16 * MIB),
        cost_estimate=pl.CostEstimate(flops=4_000_000, bytes_accessed=800_000, transcendentals=1000),
    )(msg)


def squares_of(msg_ref, out_ref):
    grad = msg_ref[...].astype(jnp.float32)
    total = jnp.sum(jnp.sum(grad * grad, axis=0), axis=0, keepdims=True)
    out_ref[...] = jnp.broadcast_to(jnp.sum(total, axis=1, keepdims=True)[None], out_ref.shape)


def squares_call(msg):
    return pl.pallas_call(
        squares_of,
        in_specs=[VMEM],
        out_specs=VMEM,
        out_shape=jax.ShapeDtypeStruct((8, 8, HD), jnp.float32),
        compiler_params=pltpu.CompilerParams(vmem_limit_bytes=16 * MIB),
        cost_estimate=pl.CostEstimate(flops=200_000, bytes_accessed=230_000, transcendentals=0),
    )(msg)


def finish(own_ref, peer_ref, sum_ref, out_ref):
    core = lax.axis_index("c")
    squares = jnp.sum(sum_ref[...], axis=0)[:1]
    factor = 1.0 / jnp.sqrt(squares / (B * QT * HQ * HD) + EPSILON)
    for ref, odd in ((own_ref, core), (peer_ref, 1 - core)):
        rows = ref[...].astype(jnp.float32) * factor
        for part in range(PARTS):
            out_ref[2 * part + odd] = rows[:, part * 8 : part * 8 + 8].reshape(QT, 32, HD).astype(jnp.bfloat16)


def finish_call(own, peer, sums):
    return pl.pallas_call(
        finish,
        in_specs=[VMEM] * 3,
        out_specs=VMEM,
        out_shape=jax.ShapeDtypeStruct((B, QT, 32, HD), jnp.bfloat16),
        compiler_params=pltpu.CompilerParams(vmem_limit_bytes=16 * MIB),
        cost_estimate=pl.CostEstimate(flops=200_000, bytes_accessed=800_000, transcendentals=0),
    )(own, peer, sums)


def local(queries, key_cache, value_cache, grad_out, cache_len):
    swap = [(0, 1), (1, 0)]
    with jax.named_scope("attend"):
        peer, own, own_st = attend_call(cache_len, queries, key_cache, value_cache, grad_out)
    with jax.named_scope("pair"):
        peer = lax.ppermute(peer, "c", swap)
        msg = pair_up_call(peer, own, own_st)
    with jax.named_scope("exchange"):
        msg = lax.all_to_all(msg, ("z", "y"), 0, 0)
    with jax.named_scope("merge"):
        msg = merge_call(msg)
    with jax.named_scope("spread"):
        msg = lax.all_to_all(msg, ("z", "y"), 0, 0)
    with jax.named_scope("norm"):
        other = lax.ppermute(msg, "c", swap)
        sums = lax.all_to_all(squares_call(msg), ("c", "x"), 0, 0)
        return finish_call(msg, other, sums)


def solution(mesh):
    fine = Mesh(mesh.devices.reshape(8, 4, 2, 4), ("z", "y", "c", "x"))
    seq = ("z", "y", "c")
    placed = (
        P(None, None, "x", None),
        P(None, seq, "x", None),
        P(None, seq, "x", None),
        P(None, None, "x", None),
        P(),
    )
    return jax.shard_map(
        local, mesh=fine, in_specs=placed, out_specs=P(None, None, "x", None), check_vma=False
    )
```

```python
import math

import jax
import jax.numpy as jnp
from jax import lax
from jax.experimental import pallas as pl
from jax.experimental.pallas import tpu as pltpu
from jax.sharding import Mesh
from jax.sharding import PartitionSpec as P

B = 6
QT = 8
HQ = 128
HD = 128

NEGATIVE = -1e30
FLOOR = -1e29
EPSILON = 1e-06
SCALE = 1.0 / math.sqrt(HD)
SCALE2 = SCALE * math.log2(math.e)
CHUNK = 256
PARTS = 3
SLOT = 56
MIB = 1024 * 1024
VMEM = pl.BlockSpec(memory_space=pltpu.VMEM)
HBM = pl.BlockSpec(memory_space=pltpu.HBM)
FIRST = (((0,), (0,)), ((), ()))


def high(x):
    return x.astype(jnp.bfloat16).astype(jnp.float32)


def attend(
    len_ref, q_hbm, k_hbm, v_hbm, go_hbm, peer_ref, own_ref, own_st_ref,
    q_buf, go_buf, k_buf, v_buf, s_a, s_b, s_c, g_a, g_b, g_c,
    d_a, d_b, d_c, f_a, f_b, f_c, f_d, sems,
):
    core = lax.axis_index("c")
    count, rows = k_buf.shape[0], k_buf.shape[1]
    span = rows // 2
    chunks = -(-span // CHUNK)
    flat = (f_a, f_b, f_c, f_d)
    start = ((lax.axis_index("z") * 4 + lax.axis_index("y")) * 2 + core) * span

    def sequence(j):
        return 2 * j + 1 - core if j < PARTS else 2 * (j - PARTS) + core

    def place(i):
        first = i * CHUNK
        return first, min(CHUNK, span - first)

    def whole(source, target, base):
        return [
            pltpu.make_async_copy(source.at[sequence(j)], target.at[j], sems.at[base + j]) for j in range(count)
        ]

    keys, values = whole(k_hbm, k_buf, 0), whole(v_hbm, v_buf, count)
    small = list(zip(whole(q_hbm, q_buf, 2 * count), whole(go_hbm, go_buf, 3 * count)))
    for j in range(count):
        for copy in (small[j][0], keys[j], small[j][1], values[j]):
            copy.start()

    scores, probs, splits = (s_a, s_b, s_c), (g_a, g_b, g_c), (d_a, d_b, d_c)
    lead = lax.broadcasted_iota(jnp.int32, (8, 256), 1) % 128 // 16 - lax.broadcasted_iota(jnp.int32, (8, 256), 0)

    def turned(x):
        blank = jnp.zeros((HD, 128), jnp.bfloat16)
        left = jnp.concatenate([x[:, :16].reshape(128, HD).T, blank], axis=0)
        right = jnp.concatenate([blank, x[:, 16:].reshape(128, HD).T], axis=0)
        return jnp.concatenate([left, right], axis=1)

    def sides(x, reduce):
        return reduce(x, axis=0, keepdims=True)

    def split(source, j, i, which):
        first, size = place(i)
        scr = flat[which * 2 + i % 2]
        scr[: 2 * size, :] = source[j, 2 * first : 2 * (first + size), :].astype(jnp.float32)
        return jnp.concatenate(
            [scr[pl.ds(side, size, stride=2), :].astype(jnp.bfloat16) for side in range(2)], axis=1
        )

    def score_step(j, i, qt, gt, room, top):
        first, size = place(i)
        at = slice(first, first + size)
        kd = split(k_buf, j, i, 0)
        splits[j % 3][at, :] = kd
        s = jnp.dot(kd, qt, preferred_element_type=jnp.float32).reshape(size // 8, 8, 256)
        tile_start = lax.broadcasted_iota(jnp.int32, (size // 8, 8, 256), 0) * 8
        s = jnp.where((room + lead - first)[None] >= tile_start, s, NEGATIVE)
        scores[j % 3][at, :] = s.reshape(size, 256)
        vd = split(v_buf, j, i, 1)
        probs[j % 3][at, :] = jnp.dot(vd, gt, preferred_element_type=jnp.float32)
        return jnp.maximum(top, jnp.max(s, axis=0))

    def weight_step(j, i, tops, total, dot):
        first, size = place(i)
        at = slice(first, first + size)
        s = scores[j % 3][at, :].reshape(size // 8, 8, 256)
        w = jnp.exp2((s - tops[None]) * SCALE2)
        scores[j % 3][at, :] = w.reshape(size, 256)
        wg = w * probs[j % 3][at, :].reshape(size // 8, 8, 256)
        return total + jnp.sum(w, axis=0), dot + jnp.sum(wg, axis=0)

    def term_step(j, i, dots, acc):
        first, size = place(i)
        at = slice(first, first + size)
        w = scores[j % 3][at, :]
        p = w * (probs[j % 3][at, :] - dots)
        out = []
        for side in range(2):
            cols = slice(side * 128, side * 128 + 128)
            pw = jnp.concatenate([p[:, cols], w[:, cols]], axis=1).astype(jnp.bfloat16)
            out.append(
                acc[side]
                + lax.dot_general(splits[j % 3][at, cols], pw, FIRST, preferred_element_type=jnp.float32)
            )
        return out

    def prepare(j):
        seq = sequence(j)
        for copy in (*small[j], keys[j], values[j]):
            copy.wait()
        return turned(q_buf[j]), turned(go_buf[j]), len_ref[seq] - QT - start

    def means_of(total, dot):
        total, dot = sides(total, jnp.sum), sides(dot, jnp.sum)
        return total, jnp.where(total > 0.0, dot / jnp.where(total > 0.0, total, 1.0), 0.0)

    def store(j, acc, tops, totals, dots):
        pieces = []
        for half in (slice(0, 128), slice(128, 256)):
            pair = [acc[side][:, half].T.reshape(8, 16, 128) for side in range(2)]
            pieces.append(jnp.concatenate(pair, axis=1).reshape(32, 8, 128))
        both = jnp.concatenate(pieces, axis=1)
        part = j % PARTS
        if j < PARTS:
            peer_ref[:, part * 16 : part * 16 + 16, :] = both.astype(jnp.bfloat16)
        else:
            own_ref[:, part * 16 : part * 16 + 16, :] = both
        sub = lax.broadcasted_iota(jnp.int32, (8, 128), 0)
        for side in range(2):
            at = slice(side * 128, side * 128 + 128)
            m, t, d = tops[:, at], totals[:, at], dots[:, at]
            cols = (m, high(t), t - high(t), high(d), d - high(d)) if j < PARTS else (m, t, d)
            block = jnp.zeros((8, 128), jnp.float32)
            for k, col in enumerate(cols):
                block = jnp.where(sub == k, col, block)
            blocks[j // PARTS, side, part] = block

    blocks = {}
    zero8 = jnp.zeros((8, 256), jnp.float32)
    stats = {}
    for n in range(count + 2):
        first, second, third = n, n - 1, n - 2
        if first < count:
            ready = prepare(first)
            top = jnp.full((8, 256), NEGATIVE, jnp.float32)
        if 0 <= second < count:
            tops = high(jnp.maximum(sides(last_top, jnp.max), FLOOR))
            total, dot = zero8, zero8
        if 0 <= third:
            acc = [jnp.zeros((128, 256), jnp.float32)] * 2
        for i in range(chunks):
            if 0 <= third:
                acc = term_step(third, i, stats[third][2], acc)
            if first < count:
                top = score_step(first, i, *ready, top)
            if 0 <= second < count:
                total, dot = weight_step(second, i, tops, total, dot)
        if 0 <= third:
            store(third, acc, *stats[third])
        if 0 <= second < count:
            stats[second] = (tops, *means_of(total, dot))
        last_top = top

    blank = jnp.zeros((8, 128), jnp.float32)
    z = jnp.concatenate(
        [blocks.get((who, side, part), blank) for who in range(2) for side in range(2) for part in range(4)], axis=0
    ).T
    for who in range(2):
        pair = []
        for side in range(2):
            shift = (128 - who * 64 - side * 32) % 128
            pair.append((pltpu.roll(z, shift, 1) if shift else z).reshape(8, 16, 128))
        st = jnp.concatenate(pair, axis=1).reshape(32, 8, 128)
        if who == 0:
            peer_ref[:, 48:64, :] = jnp.concatenate([st, jnp.zeros_like(st)], axis=1).astype(jnp.bfloat16)
        else:
            own_st_ref[...] = st


def attend_call(lengths, q, k, v, go):
    count, span = k.shape[0], k.shape[1]
    q, k, v, go = (
        pltpu.with_memory_space_constraint(x, pltpu.HBM)
        for x in (q, k.reshape(count, span * 2, HD), v.reshape(count, span * 2, HD), go)
    )
    wide = pltpu.VMEM((span, 256), jnp.float32)
    slim = pltpu.VMEM((span, 256), jnp.bfloat16)
    flat = pltpu.VMEM((2 * CHUNK, HD), jnp.float32)
    return pl.pallas_call(
        attend,
        in_specs=[pl.BlockSpec(memory_space=pltpu.SMEM), HBM, HBM, HBM, HBM],
        out_specs=[VMEM, VMEM, VMEM],
        out_shape=[
            pltpu.VMEM((32, 64, HD), jnp.bfloat16),
            pltpu.VMEM((32, 48, HD), jnp.float32),
            pltpu.VMEM((32, 8, HD), jnp.float32),
        ],
        scratch_shapes=[
            pltpu.VMEM(q.shape, jnp.bfloat16),
            pltpu.VMEM(go.shape, jnp.bfloat16),
            pltpu.VMEM(k.shape, jnp.bfloat16),
            pltpu.VMEM(v.shape, jnp.bfloat16),
            wide, wide, wide, wide, wide, wide, slim, slim, slim, flat, flat, flat, flat,
            pltpu.SemaphoreType.DMA((4 * count,)),
        ],
        compiler_params=pltpu.CompilerParams(vmem_limit_bytes=56 * MIB),
        cost_estimate=pl.CostEstimate(flops=4_500_000_000, bytes_accessed=14_000_000, transcendentals=3_000_000),
    )(lengths, q, k, v, go)


def column(st, part, k):
    at = 8 * part + k
    return st[:, :, at : at + 1]


def pair_up(peer_ref, own_ref, own_st_ref, out_ref):
    peer = peer_ref[...].astype(jnp.float32)
    own = own_ref[...]
    peer_st, own_st = peer[:, 48:56], own_st_ref[...]
    lane = lax.broadcasted_iota(jnp.int32, (32, 8, 128), 2)
    st = jnp.zeros((32, 8, 128), jnp.float32)
    pieces = []
    for part in range(PARTS):
        at = part * 16
        top_a, total_a, dot_a = (column(own_st, part, k) for k in range(3))
        top_b = column(peer_st, part, 0)
        total_b = column(peer_st, part, 1) + column(peer_st, part, 2)
        dot_b = column(peer_st, part, 3) + column(peer_st, part, 4)
        top = jnp.maximum(top_a, top_b)
        factor_a = jnp.exp2((top_a - top) * SCALE2)
        factor_b = jnp.exp2((top_b - top) * SCALE2)
        total_a, total_b = factor_a * total_a, factor_b * total_b
        total = total_a + total_b
        dot = (total_a * dot_a + total_b * dot_b) / jnp.where(total > 0.0, total, 1.0)
        term_a, term_b = own[:, at : at + 8], peer[:, at : at + 8]
        mass_a, mass_b = own[:, at + 8 : at + 16], peer[:, at + 8 : at + 16]
        pieces.append(
            factor_a * term_a + (factor_a * (dot_a - dot)) * mass_a
            + (factor_b * term_b + (factor_b * (dot_b - dot)) * mass_b)
        )
        pieces.append(factor_a * mass_a + factor_b * mass_b)
        for k, col in enumerate((top, high(total), total - high(total), high(dot), dot - high(dot))):
            st = jnp.where(lane == 8 * part + k, col, st)
    out_ref[...] = jnp.concatenate(pieces + [st], axis=1).astype(jnp.bfloat16)


def pair_up_call(peer, own, own_st):
    return pl.pallas_call(
        pair_up,
        in_specs=[VMEM] * 3,
        out_specs=VMEM,
        out_shape=jax.ShapeDtypeStruct((32, SLOT, HD), jnp.bfloat16),
        compiler_params=pltpu.CompilerParams(vmem_limit_bytes=24 * MIB),
        cost_estimate=pl.CostEstimate(flops=4_000_000, bytes_accessed=2_000_000, transcendentals=1000),
    )(peer, own, own_st)


def merge(msg_ref, out_ref):
    msg = msg_ref[...].astype(jnp.float32)
    st = msg[:, 48:56]
    rows = []
    for part in range(PARTS):
        at = part * 16
        top = column(st, part, 0)
        total = column(st, part, 1) + column(st, part, 2)
        dot = column(st, part, 3) + column(st, part, 4)
        factor = jnp.exp2((top - jnp.max(top, axis=0, keepdims=True)) * SCALE2)
        total = factor * total
        whole = jnp.sum(total, axis=0, keepdims=True)
        mean = jnp.sum(total * dot, axis=0, keepdims=True) / whole
        grad = jnp.sum(factor * msg[:, at : at + 8] + (factor * (dot - mean)) * msg[:, at + 8 : at + 16], axis=0)
        rows.append(grad * (SCALE / whole[0]))
    block = jnp.concatenate(rows, axis=0).astype(jnp.bfloat16)
    out_ref[...] = jnp.broadcast_to(block[None], out_ref.shape)


def merge_call(msg):
    return pl.pallas_call(
        merge,
        in_specs=[VMEM],
        out_specs=VMEM,
        out_shape=jax.ShapeDtypeStruct((32, 8 * PARTS, HD), jnp.bfloat16),
        compiler_params=pltpu.CompilerParams(vmem_limit_bytes=16 * MIB),
        cost_estimate=pl.CostEstimate(flops=4_000_000, bytes_accessed=800_000, transcendentals=1000),
    )(msg)


def squares_of(msg_ref, out_ref):
    grad = msg_ref[...].astype(jnp.float32)
    total = jnp.sum(jnp.sum(grad * grad, axis=0), axis=0, keepdims=True)
    out_ref[...] = jnp.broadcast_to(jnp.sum(total, axis=1, keepdims=True)[None], out_ref.shape)


def squares_call(msg):
    return pl.pallas_call(
        squares_of,
        in_specs=[VMEM],
        out_specs=VMEM,
        out_shape=jax.ShapeDtypeStruct((8, 8, HD), jnp.float32),
        compiler_params=pltpu.CompilerParams(vmem_limit_bytes=16 * MIB),
        cost_estimate=pl.CostEstimate(flops=200_000, bytes_accessed=230_000, transcendentals=0),
    )(msg)


def finish(own_ref, peer_ref, sum_ref, out_ref):
    core = lax.axis_index("c")
    squares = jnp.sum(sum_ref[...], axis=0)[:1]
    factor = 1.0 / jnp.sqrt(squares / (B * QT * HQ * HD) + EPSILON)
    for ref, odd in ((own_ref, core), (peer_ref, 1 - core)):
        rows = ref[...].astype(jnp.float32) * factor
        for part in range(PARTS):
            out_ref[2 * part + odd] = rows[:, part * 8 : part * 8 + 8].reshape(QT, 32, HD).astype(jnp.bfloat16)


def finish_call(own, peer, sums):
    return pl.pallas_call(
        finish,
        in_specs=[VMEM] * 3,
        out_specs=VMEM,
        out_shape=jax.ShapeDtypeStruct((B, QT, 32, HD), jnp.bfloat16),
        compiler_params=pltpu.CompilerParams(vmem_limit_bytes=16 * MIB),
        cost_estimate=pl.CostEstimate(flops=200_000, bytes_accessed=800_000, transcendentals=0),
    )(own, peer, sums)


def local(queries, key_cache, value_cache, grad_out, cache_len):
    swap = [(0, 1), (1, 0)]
    with jax.named_scope("attend"):
        peer, own, own_st = attend_call(cache_len, queries, key_cache, value_cache, grad_out)
    with jax.named_scope("pair"):
        peer = lax.ppermute(peer, "c", swap)
        msg = pair_up_call(peer, own, own_st)
    with jax.named_scope("exchange"):
        msg = lax.all_to_all(msg, ("z", "y"), 0, 0)
    with jax.named_scope("merge"):
        msg = merge_call(msg)
    with jax.named_scope("spread"):
        msg = lax.all_to_all(msg, ("z", "y"), 0, 0)
    with jax.named_scope("norm"):
        other = lax.ppermute(msg, "c", swap)
        sums = lax.all_to_all(squares_call(msg), ("c", "x"), 0, 0)
        return finish_call(msg, other, sums)


def solution(mesh):
    fine = Mesh(mesh.devices.reshape(8, 4, 2, 4), ("z", "y", "c", "x"))
    seq = ("z", "y", "c")
    placed = (
        P(None, None, "x", None),
        P(None, seq, "x", None),
        P(None, seq, "x", None),
        P(None, None, "x", None),
        P(),
    )
    return jax.shard_map(
        local, mesh=fine, in_specs=placed, out_specs=P(None, None, "x", None), check_vma=False
    )
```

```python
import math

import jax
import jax.numpy as jnp
from jax import lax
from jax.experimental import pallas as pl
from jax.experimental.pallas import tpu as pltpu
from jax.sharding import Mesh
from jax.sharding import PartitionSpec as P

B = 6
QT = 8
HQ = 128
HD = 128

NEGATIVE = -1e30
FLOOR = -1e29
EPSILON = 1e-06
SCALE = 1.0 / math.sqrt(HD)
SCALE2 = SCALE * math.log2(math.e)
CHUNK = 256
PARTS = 3
SLOT = 56
MIB = 1024 * 1024
VMEM = pl.BlockSpec(memory_space=pltpu.VMEM)
HBM = pl.BlockSpec(memory_space=pltpu.HBM)
FIRST = (((0,), (0,)), ((), ()))


def high(x):
    return x.astype(jnp.bfloat16).astype(jnp.float32)


def attend(
    len_ref, q_hbm, k_hbm, v_hbm, go_hbm, peer_ref, own_ref, own_st_ref,
    q_buf, go_buf, k_buf, v_buf, s_a, s_b, s_c, g_a, g_b, g_c,
    d_a, d_b, d_c, f_a, f_b, f_c, f_d, sems,
):
    core = lax.axis_index("c")
    count, rows = k_buf.shape[0], k_buf.shape[1]
    span = rows // 2
    chunks = -(-span // CHUNK)
    flat = (f_a, f_b, f_c, f_d)
    start = ((lax.axis_index("z") * 4 + lax.axis_index("y")) * 2 + core) * span

    def sequence(j):
        return 2 * j + 1 - core if j < PARTS else 2 * (j - PARTS) + core

    def place(i):
        first = i * CHUNK
        return first, min(CHUNK, span - first)

    def whole(source, target, base):
        return [
            pltpu.make_async_copy(source.at[sequence(j)], target.at[j], sems.at[base + j]) for j in range(count)
        ]

    keys, values = whole(k_hbm, k_buf, 0), whole(v_hbm, v_buf, count)
    small = list(zip(whole(q_hbm, q_buf, 2 * count), whole(go_hbm, go_buf, 3 * count)))
    for j in range(count):
        for copy in (small[j][0], keys[j], small[j][1], values[j]):
            copy.start()

    scores, probs, splits = (s_a, s_b, s_c), (g_a, g_b, g_c), (d_a, d_b, d_c)
    lead = lax.broadcasted_iota(jnp.int32, (8, 128), 1) // 16 - lax.broadcasted_iota(jnp.int32, (8, 128), 0)

    def turned(x):
        blank = jnp.zeros((HD, 128), jnp.bfloat16)
        left = jnp.concatenate([x[:, :16].reshape(128, HD).T, blank], axis=0)
        right = jnp.concatenate([blank, x[:, 16:].reshape(128, HD).T], axis=0)
        return jnp.concatenate([left, right], axis=1)

    def sides(x, reduce):
        return reduce(x, axis=0, keepdims=True)

    def split(source, j, i, which):
        first, size = place(i)
        scr = flat[which * 2 + i % 2]
        scr[: 2 * size, :] = source[j, 2 * first : 2 * (first + size), :].astype(jnp.float32)
        return jnp.concatenate(
            [scr[pl.ds(side, size, stride=2), :].astype(jnp.bfloat16) for side in range(2)], axis=1
        )

    def score_step(j, i, qt, gt, room, top):
        first, size = place(i)
        at = slice(first, first + size)
        kd = split(k_buf, j, i, 0)
        splits[j % 3][at, :] = kd
        s = jnp.dot(kd, qt, preferred_element_type=jnp.float32)
        tile_start = lax.broadcasted_iota(jnp.int32, (size // 8, 8, 128), 0) * 8
        visible = (room + lead - first)[None] >= tile_start
        peaks = []
        for side in range(2):
            cols = slice(side * 128, side * 128 + 128)
            half = jnp.where(visible, s[:, cols].reshape(size // 8, 8, 128), NEGATIVE)
            scores[j % 3][at, cols] = half.reshape(size, 128)
            peaks.append(jnp.max(half, axis=0))
        vd = split(v_buf, j, i, 1)
        probs[j % 3][at, :] = jnp.dot(vd, gt, preferred_element_type=jnp.float32)
        return jnp.maximum(top, jnp.concatenate(peaks, axis=1))

    def weight_step(j, i, tops, total, dot):
        first, size = place(i)
        at = slice(first, first + size)
        s = scores[j % 3][at, :].reshape(size // 8, 8, 256)
        w = jnp.exp2((s - tops[None]) * SCALE2)
        scores[j % 3][at, :] = w.reshape(size, 256)
        wg = w * probs[j % 3][at, :].reshape(size // 8, 8, 256)
        return total + jnp.sum(w, axis=0), dot + jnp.sum(wg, axis=0)

    def term_step(j, i, dots, acc):
        first, size = place(i)
        at = slice(first, first + size)
        w = scores[j % 3][at, :]
        p = w * (probs[j % 3][at, :] - dots)
        out = []
        for side in range(2):
            cols = slice(side * 128, side * 128 + 128)
            pw = jnp.concatenate([p[:, cols], w[:, cols]], axis=1).astype(jnp.bfloat16)
            out.append(
                acc[side]
                + lax.dot_general(splits[j % 3][at, cols], pw, FIRST, preferred_element_type=jnp.float32)
            )
        return out

    def prepare(j):
        seq = sequence(j)
        for copy in (*small[j], keys[j], values[j]):
            copy.wait()
        return turned(q_buf[j]), turned(go_buf[j]), len_ref[seq] - QT - start

    def means_of(total, dot):
        total, dot = sides(total, jnp.sum), sides(dot, jnp.sum)
        return total, jnp.where(total > 0.0, dot / jnp.where(total > 0.0, total, 1.0), 0.0)

    def store(j, acc, tops, totals, dots):
        pieces = []
        for half in (slice(0, 128), slice(128, 256)):
            pair = [acc[side][:, half].T.reshape(8, 16, 128) for side in range(2)]
            pieces.append(jnp.concatenate(pair, axis=1).reshape(32, 8, 128))
        both = jnp.concatenate(pieces, axis=1)
        part = j % PARTS
        if j < PARTS:
            peer_ref[:, part * 16 : part * 16 + 16, :] = both.astype(jnp.bfloat16)
        else:
            own_ref[:, part * 16 : part * 16 + 16, :] = both
        sub = lax.broadcasted_iota(jnp.int32, (8, 128), 0)
        for side in range(2):
            at = slice(side * 128, side * 128 + 128)
            m, t, d = tops[:, at], totals[:, at], dots[:, at]
            cols = (m, high(t), t - high(t), high(d), d - high(d)) if j < PARTS else (m, t, d)
            block = jnp.zeros((8, 128), jnp.float32)
            for k, col in enumerate(cols):
                block = jnp.where(sub == k, col, block)
            blocks[j // PARTS, side, part] = block

    blocks = {}
    zero8 = jnp.zeros((8, 256), jnp.float32)
    stats = {}
    for n in range(count + 2):
        first, second, third = n, n - 1, n - 2
        if first < count:
            ready = prepare(first)
            top = jnp.full((8, 256), NEGATIVE, jnp.float32)
        if 0 <= second < count:
            tops = high(jnp.maximum(sides(last_top, jnp.max), FLOOR))
            total, dot = zero8, zero8
        if 0 <= third:
            acc = [jnp.zeros((128, 256), jnp.float32)] * 2
        for i in range(chunks):
            if 0 <= third:
                acc = term_step(third, i, stats[third][2], acc)
            if first < count:
                top = score_step(first, i, *ready, top)
            if 0 <= second < count:
                total, dot = weight_step(second, i, tops, total, dot)
        if 0 <= third:
            store(third, acc, *stats[third])
        if 0 <= second < count:
            stats[second] = (tops, *means_of(total, dot))
        last_top = top

    blank = jnp.zeros((8, 128), jnp.float32)
    z = jnp.concatenate(
        [blocks.get((who, side, part), blank) for who in range(2) for side in range(2) for part in range(4)], axis=0
    ).T
    for who in range(2):
        pair = []
        for side in range(2):
            shift = (128 - who * 64 - side * 32) % 128
            pair.append((pltpu.roll(z, shift, 1) if shift else z).reshape(8, 16, 128))
        st = jnp.concatenate(pair, axis=1).reshape(32, 8, 128)
        if who == 0:
            peer_ref[:, 48:64, :] = jnp.concatenate([st, jnp.zeros_like(st)], axis=1).astype(jnp.bfloat16)
        else:
            own_st_ref[...] = st


def attend_call(lengths, q, k, v, go):
    count, span = k.shape[0], k.shape[1]
    q, k, v, go = (
        pltpu.with_memory_space_constraint(x, pltpu.HBM)
        for x in (q, k.reshape(count, span * 2, HD), v.reshape(count, span * 2, HD), go)
    )
    wide = pltpu.VMEM((span, 256), jnp.float32)
    slim = pltpu.VMEM((span, 256), jnp.bfloat16)
    flat = pltpu.VMEM((2 * CHUNK, HD), jnp.float32)
    return pl.pallas_call(
        attend,
        in_specs=[pl.BlockSpec(memory_space=pltpu.SMEM), HBM, HBM, HBM, HBM],
        out_specs=[VMEM, VMEM, VMEM],
        out_shape=[
            pltpu.VMEM((32, 64, HD), jnp.bfloat16),
            pltpu.VMEM((32, 48, HD), jnp.float32),
            pltpu.VMEM((32, 8, HD), jnp.float32),
        ],
        scratch_shapes=[
            pltpu.VMEM(q.shape, jnp.bfloat16),
            pltpu.VMEM(go.shape, jnp.bfloat16),
            pltpu.VMEM(k.shape, jnp.bfloat16),
            pltpu.VMEM(v.shape, jnp.bfloat16),
            wide, wide, wide, wide, wide, wide, slim, slim, slim, flat, flat, flat, flat,
            pltpu.SemaphoreType.DMA((4 * count,)),
        ],
        compiler_params=pltpu.CompilerParams(vmem_limit_bytes=56 * MIB),
        cost_estimate=pl.CostEstimate(flops=4_500_000_000, bytes_accessed=14_000_000, transcendentals=3_000_000),
    )(lengths, q, k, v, go)


def shifted(st, k):
    return pltpu.roll(st.reshape(256, 128), 128 - k, 1).reshape(32, 8, 128)


def spread_stats(st):
    return st, shifted(st, 1) + shifted(st, 2), shifted(st, 3) + shifted(st, 4)


def column(x, part):
    return x[..., 8 * part : 8 * part + 1]


def pair_up(peer_ref, own_ref, own_st_ref, out_ref):
    peer = peer_ref[...].astype(jnp.float32)
    own = own_ref[...]
    own_st = own_st_ref[...]
    top_a, total_a, dot_a = own_st, shifted(own_st, 1), shifted(own_st, 2)
    top_b, total_b, dot_b = spread_stats(peer[:, 48:56])
    top = jnp.maximum(top_a, top_b)
    factor_a = jnp.exp2((top_a - top) * SCALE2)
    factor_b = jnp.exp2((top_b - top) * SCALE2)
    total_a, total_b = factor_a * total_a, factor_b * total_b
    total = total_a + total_b
    dot = (total_a * dot_a + total_b * dot_b) / jnp.where(total > 0.0, total, 1.0)
    lag_a, lag_b = factor_a * (dot_a - dot), factor_b * (dot_b - dot)
    pieces = []
    for part in range(PARTS):
        at = part * 16
        term_a, term_b = own[:, at : at + 8], peer[:, at : at + 8]
        mass_a, mass_b = own[:, at + 8 : at + 16], peer[:, at + 8 : at + 16]
        take_a, take_b = column(factor_a, part), column(factor_b, part)
        pieces.append(
            take_a * term_a + column(lag_a, part) * mass_a + (take_b * term_b + column(lag_b, part) * mass_b)
        )
        pieces.append(take_a * mass_a + take_b * mass_b)
    lane = lax.broadcasted_iota(jnp.int32, (32, 8, 128), 2)
    st = jnp.zeros((32, 8, 128), jnp.float32)
    for k, value in enumerate((top, high(total), total - high(total), high(dot), dot - high(dot))):
        st = jnp.where((lane % 8 == k) & (lane < 8 * PARTS), shifted(value, 128 - k) if k else value, st)
    out_ref[...] = jnp.concatenate(pieces + [st], axis=1).astype(jnp.bfloat16)


def pair_up_call(peer, own, own_st):
    return pl.pallas_call(
        pair_up,
        in_specs=[VMEM] * 3,
        out_specs=VMEM,
        out_shape=jax.ShapeDtypeStruct((32, SLOT, HD), jnp.bfloat16),
        compiler_params=pltpu.CompilerParams(vmem_limit_bytes=24 * MIB),
        cost_estimate=pl.CostEstimate(flops=4_000_000, bytes_accessed=2_000_000, transcendentals=1000),
    )(peer, own, own_st)


def merge(msg_ref, out_ref):
    msg = msg_ref[...].astype(jnp.float32)
    top, total, dot = spread_stats(msg[:, 48:56])
    factor = jnp.exp2((top - jnp.max(top, axis=0, keepdims=True)) * SCALE2)
    total = factor * total
    whole = jnp.sum(total, axis=0, keepdims=True)
    lag = factor * (dot - jnp.sum(total * dot, axis=0, keepdims=True) / whole)
    scale = (SCALE / whole)[0]
    rows = []
    for part in range(PARTS):
        at = part * 16
        grad = jnp.sum(
            column(factor, part) * msg[:, at : at + 8] + column(lag, part) * msg[:, at + 8 : at + 16], axis=0
        )
        rows.append(grad * column(scale, part))
    block = jnp.concatenate(rows, axis=0).astype(jnp.bfloat16)
    out_ref[...] = jnp.broadcast_to(block[None], out_ref.shape)


def merge_call(msg):
    return pl.pallas_call(
        merge,
        in_specs=[VMEM],
        out_specs=VMEM,
        out_shape=jax.ShapeDtypeStruct((32, 8 * PARTS, HD), jnp.bfloat16),
        compiler_params=pltpu.CompilerParams(vmem_limit_bytes=16 * MIB),
        cost_estimate=pl.CostEstimate(flops=4_000_000, bytes_accessed=800_000, transcendentals=1000),
    )(msg)


def squares_of(msg_ref, out_ref):
    grad = msg_ref[...].astype(jnp.float32)
    total = jnp.sum(jnp.sum(grad * grad, axis=0), axis=0, keepdims=True)
    out_ref[...] = jnp.broadcast_to(jnp.sum(total, axis=1, keepdims=True)[None], out_ref.shape)


def squares_call(msg):
    return pl.pallas_call(
        squares_of,
        in_specs=[VMEM],
        out_specs=VMEM,
        out_shape=jax.ShapeDtypeStruct((8, 8, HD), jnp.float32),
        compiler_params=pltpu.CompilerParams(vmem_limit_bytes=16 * MIB),
        cost_estimate=pl.CostEstimate(flops=200_000, bytes_accessed=230_000, transcendentals=0),
    )(msg)


def finish(own_ref, peer_ref, sum_ref, out_ref):
    core = lax.axis_index("c")
    squares = jnp.sum(sum_ref[...], axis=0)[:1]
    factor = 1.0 / jnp.sqrt(squares / (B * QT * HQ * HD) + EPSILON)
    for ref, odd in ((own_ref, core), (peer_ref, 1 - core)):
        rows = ref[...].astype(jnp.float32) * factor
        for part in range(PARTS):
            out_ref[2 * part + odd] = rows[:, part * 8 : part * 8 + 8].reshape(QT, 32, HD).astype(jnp.bfloat16)


def finish_call(own, peer, sums):
    return pl.pallas_call(
        finish,
        in_specs=[VMEM] * 3,
        out_specs=VMEM,
        out_shape=jax.ShapeDtypeStruct((B, QT, 32, HD), jnp.bfloat16),
        compiler_params=pltpu.CompilerParams(vmem_limit_bytes=16 * MIB),
        cost_estimate=pl.CostEstimate(flops=200_000, bytes_accessed=800_000, transcendentals=0),
    )(own, peer, sums)


def local(queries, key_cache, value_cache, grad_out, cache_len):
    swap = [(0, 1), (1, 0)]
    with jax.named_scope("attend"):
        peer, own, own_st = attend_call(cache_len, queries, key_cache, value_cache, grad_out)
    with jax.named_scope("pair"):
        peer = lax.ppermute(peer, "c", swap)
        msg = pair_up_call(peer, own, own_st)
    with jax.named_scope("exchange"):
        msg = lax.all_to_all(msg, ("z", "y"), 0, 0)
    with jax.named_scope("merge"):
        msg = merge_call(msg)
    with jax.named_scope("spread"):
        msg = lax.all_to_all(msg, ("z", "y"), 0, 0)
    with jax.named_scope("norm"):
        other = lax.ppermute(msg, "c", swap)
        sums = lax.all_to_all(squares_call(msg), ("c", "x"), 0, 0)
        return finish_call(msg, other, sums)


def solution(mesh):
    fine = Mesh(mesh.devices.reshape(8, 4, 2, 4), ("z", "y", "c", "x"))
    seq = ("z", "y", "c")
    placed = (
        P(None, None, "x", None),
        P(None, seq, "x", None),
        P(None, seq, "x", None),
        P(None, None, "x", None),
        P(),
    )
    return jax.shard_map(
        local, mesh=fine, in_specs=placed, out_specs=P(None, None, "x", None), check_vma=False
    )
```

```python
import math

import jax
import jax.numpy as jnp
from jax import lax
from jax.experimental import pallas as pl
from jax.experimental.pallas import tpu as pltpu
from jax.sharding import Mesh
from jax.sharding import PartitionSpec as P

B = 6
QT = 8
HQ = 128
HD = 128

NEGATIVE = -1e30
FLOOR = -1e29
EPSILON = 1e-06
SCALE = 1.0 / math.sqrt(HD)
SCALE2 = SCALE * math.log2(math.e)
CHUNK = 256
PARTS = 3
SLOT = 56
MIB = 1024 * 1024
VMEM = pl.BlockSpec(memory_space=pltpu.VMEM)
HBM = pl.BlockSpec(memory_space=pltpu.HBM)
FIRST = (((0,), (0,)), ((), ()))


def high(x):
    return x.astype(jnp.bfloat16).astype(jnp.float32)


def attend(
    len_ref, q_hbm, k_hbm, v_hbm, go_hbm, peer_ref, own_ref, own_st_ref,
    q_buf, go_buf, k_buf, v_buf, s_a, s_b, s_c, g_a, g_b, g_c,
    d_a, d_b, d_c, sems,
):
    core = lax.axis_index("c")
    count, rows = k_buf.shape[0], k_buf.shape[1]
    span = rows // 2
    chunks = -(-span // CHUNK)
    start = ((lax.axis_index("z") * 4 + lax.axis_index("y")) * 2 + core) * span

    def sequence(j):
        return 2 * j + 1 - core if j < PARTS else 2 * (j - PARTS) + core

    def place(i):
        first = i * CHUNK
        return first, min(CHUNK, span - first)

    def whole(source, target, base):
        return [
            pltpu.make_async_copy(source.at[sequence(j)], target.at[j], sems.at[base + j]) for j in range(count)
        ]

    keys, values = whole(k_hbm, k_buf, 0), whole(v_hbm, v_buf, count)
    small = list(zip(whole(q_hbm, q_buf, 2 * count), whole(go_hbm, go_buf, 3 * count)))
    for j in range(count):
        for copy in (small[j][0], keys[j], small[j][1], values[j]):
            copy.start()

    scores, probs, splits = (s_a, s_b, s_c), (g_a, g_b, g_c), (d_a, d_b, d_c)
    lead = lax.broadcasted_iota(jnp.int32, (8, 128), 1) // 16 - lax.broadcasted_iota(jnp.int32, (8, 128), 0)

    def turned(x):
        blank = jnp.zeros((HD, 128), jnp.bfloat16)
        left = jnp.concatenate([x[:, :16].reshape(128, HD).T, blank], axis=0)
        right = jnp.concatenate([blank, x[:, 16:].reshape(128, HD).T], axis=0)
        return jnp.concatenate([left, right], axis=1)

    def sides(x, reduce):
        return reduce(x, axis=0, keepdims=True)

    def split(source, j, i):
        first, size = place(i)
        return source[j, 2 * first : 2 * (first + size), :].reshape(size, 2 * HD)

    def score_step(j, i, qt, gt, room, top):
        first, size = place(i)
        at = slice(first, first + size)
        kd = split(k_buf, j, i)
        splits[j % 3][at, :] = kd
        s = jnp.dot(kd, qt, preferred_element_type=jnp.float32)
        tile_start = lax.broadcasted_iota(jnp.int32, (size // 8, 8, 128), 0) * 8
        visible = (room + lead - first)[None] >= tile_start
        peaks = []
        for side in range(2):
            cols = slice(side * 128, side * 128 + 128)
            half = jnp.where(visible, s[:, cols].reshape(size // 8, 8, 128), NEGATIVE)
            scores[j % 3][at, cols] = half.reshape(size, 128)
            peaks.append(jnp.max(half, axis=0))
        vd = split(v_buf, j, i)
        probs[j % 3][at, :] = jnp.dot(vd, gt, preferred_element_type=jnp.float32)
        return jnp.maximum(top, jnp.concatenate(peaks, axis=1))

    def weight_step(j, i, tops, total, dot):
        first, size = place(i)
        at = slice(first, first + size)
        s = scores[j % 3][at, :].reshape(size // 8, 8, 256)
        w = jnp.exp2((s - tops[None]) * SCALE2)
        scores[j % 3][at, :] = w.reshape(size, 256)
        wg = w * probs[j % 3][at, :].reshape(size // 8, 8, 256)
        return total + jnp.sum(w, axis=0), dot + jnp.sum(wg, axis=0)

    def term_step(j, i, dots, acc):
        first, size = place(i)
        at = slice(first, first + size)
        w = scores[j % 3][at, :]
        p = w * (probs[j % 3][at, :] - dots)
        out = []
        for side in range(2):
            cols = slice(side * 128, side * 128 + 128)
            pw = jnp.concatenate([p[:, cols], w[:, cols]], axis=1).astype(jnp.bfloat16)
            out.append(
                acc[side]
                + lax.dot_general(splits[j % 3][at, cols], pw, FIRST, preferred_element_type=jnp.float32)
            )
        return out

    def prepare(j):
        seq = sequence(j)
        for copy in (*small[j], keys[j], values[j]):
            copy.wait()
        return turned(q_buf[j]), turned(go_buf[j]), len_ref[seq] - QT - start

    def means_of(total, dot):
        total, dot = sides(total, jnp.sum), sides(dot, jnp.sum)
        return total, jnp.where(total > 0.0, dot / jnp.where(total > 0.0, total, 1.0), 0.0)

    def store(j, acc, tops, totals, dots):
        pieces = []
        for half in (slice(0, 128), slice(128, 256)):
            pair = [acc[side][:, half].T.reshape(8, 16, 128) for side in range(2)]
            pieces.append(jnp.concatenate(pair, axis=1).reshape(32, 8, 128))
        both = jnp.concatenate(pieces, axis=1)
        part = j % PARTS
        if j < PARTS:
            peer_ref[:, part * 16 : part * 16 + 16, :] = both.astype(jnp.bfloat16)
        else:
            own_ref[:, part * 16 : part * 16 + 16, :] = both
        sub = lax.broadcasted_iota(jnp.int32, (8, 128), 0)
        for side in range(2):
            at = slice(side * 128, side * 128 + 128)
            m, t, d = tops[:, at], totals[:, at], dots[:, at]
            cols = (m, high(t), t - high(t), high(d), d - high(d)) if j < PARTS else (m, t, d)
            block = jnp.zeros((8, 128), jnp.float32)
            for k, col in enumerate(cols):
                block = jnp.where(sub == k, col, block)
            blocks[j // PARTS, side, part] = block

    blocks = {}
    zero8 = jnp.zeros((8, 256), jnp.float32)
    stats = {}
    for n in range(count + 2):
        first, second, third = n, n - 1, n - 2
        if first < count:
            ready = prepare(first)
            top = jnp.full((8, 256), NEGATIVE, jnp.float32)
        if 0 <= second < count:
            tops = high(jnp.maximum(sides(last_top, jnp.max), FLOOR))
            total, dot = zero8, zero8
        if 0 <= third:
            acc = [jnp.zeros((128, 256), jnp.float32)] * 2
        for i in range(chunks):
            if 0 <= third:
                acc = term_step(third, i, stats[third][2], acc)
            if first < count:
                top = score_step(first, i, *ready, top)
            if 0 <= second < count:
                total, dot = weight_step(second, i, tops, total, dot)
        if 0 <= third:
            store(third, acc, *stats[third])
        if 0 <= second < count:
            stats[second] = (tops, *means_of(total, dot))
        last_top = top

    blank = jnp.zeros((8, 128), jnp.float32)
    z = jnp.concatenate(
        [blocks.get((who, side, part), blank) for who in range(2) for side in range(2) for part in range(4)], axis=0
    ).T
    for who in range(2):
        pair = []
        for side in range(2):
            shift = (128 - who * 64 - side * 32) % 128
            pair.append((pltpu.roll(z, shift, 1) if shift else z).reshape(8, 16, 128))
        st = jnp.concatenate(pair, axis=1).reshape(32, 8, 128)
        if who == 0:
            peer_ref[:, 48:64, :] = jnp.concatenate([st, jnp.zeros_like(st)], axis=1).astype(jnp.bfloat16)
        else:
            own_st_ref[...] = st


def attend_call(lengths, q, k, v, go):
    count, span = k.shape[0], k.shape[1]
    q, k, v, go = (
        pltpu.with_memory_space_constraint(x, pltpu.HBM)
        for x in (q, k.reshape(count, span * 2, HD), v.reshape(count, span * 2, HD), go)
    )
    wide = pltpu.VMEM((span, 256), jnp.float32)
    slim = pltpu.VMEM((span, 256), jnp.bfloat16)
    return pl.pallas_call(
        attend,
        in_specs=[pl.BlockSpec(memory_space=pltpu.SMEM), HBM, HBM, HBM, HBM],
        out_specs=[VMEM, VMEM, VMEM],
        out_shape=[
            pltpu.VMEM((32, 64, HD), jnp.bfloat16),
            pltpu.VMEM((32, 48, HD), jnp.float32),
            pltpu.VMEM((32, 8, HD), jnp.float32),
        ],
        scratch_shapes=[
            pltpu.VMEM(q.shape, jnp.bfloat16),
            pltpu.VMEM(go.shape, jnp.bfloat16),
            pltpu.VMEM(k.shape, jnp.bfloat16),
            pltpu.VMEM(v.shape, jnp.bfloat16),
            wide, wide, wide, wide, wide, wide, slim, slim, slim,
            pltpu.SemaphoreType.DMA((4 * count,)),
        ],
        compiler_params=pltpu.CompilerParams(vmem_limit_bytes=56 * MIB),
        cost_estimate=pl.CostEstimate(flops=4_500_000_000, bytes_accessed=14_000_000, transcendentals=3_000_000),
    )(lengths, q, k, v, go)


def shifted(st, k):
    return pltpu.roll(st.reshape(256, 128), 128 - k, 1).reshape(32, 8, 128)


def spread_stats(st):
    return st, shifted(st, 1) + shifted(st, 2), shifted(st, 3) + shifted(st, 4)


def column(x, part):
    return x[..., 8 * part : 8 * part + 1]


def pair_up(peer_ref, own_ref, own_st_ref, out_ref):
    peer = peer_ref[...].astype(jnp.float32)
    own = own_ref[...]
    own_st = own_st_ref[...]
    top_a, total_a, dot_a = own_st, shifted(own_st, 1), shifted(own_st, 2)
    top_b, total_b, dot_b = spread_stats(peer[:, 48:56])
    top = jnp.maximum(top_a, top_b)
    factor_a = jnp.exp2((top_a - top) * SCALE2)
    factor_b = jnp.exp2((top_b - top) * SCALE2)
    total_a, total_b = factor_a * total_a, factor_b * total_b
    total = total_a + total_b
    dot = (total_a * dot_a + total_b * dot_b) / jnp.where(total > 0.0, total, 1.0)
    lag_a, lag_b = factor_a * (dot_a - dot), factor_b * (dot_b - dot)
    pieces = []
    for part in range(PARTS):
        at = part * 16
        term_a, term_b = own[:, at : at + 8], peer[:, at : at + 8]
        mass_a, mass_b = own[:, at + 8 : at + 16], peer[:, at + 8 : at + 16]
        take_a, take_b = column(factor_a, part), column(factor_b, part)
        pieces.append(
            take_a * term_a + column(lag_a, part) * mass_a + (take_b * term_b + column(lag_b, part) * mass_b)
        )
        pieces.append(take_a * mass_a + take_b * mass_b)
    lane = lax.broadcasted_iota(jnp.int32, (32, 8, 128), 2)
    st = jnp.zeros((32, 8, 128), jnp.float32)
    for k, value in enumerate((top, high(total), total - high(total), high(dot), dot - high(dot))):
        st = jnp.where((lane % 8 == k) & (lane < 8 * PARTS), shifted(value, 128 - k) if k else value, st)
    out_ref[...] = jnp.concatenate(pieces + [st], axis=1).astype(jnp.bfloat16)


def pair_up_call(peer, own, own_st):
    return pl.pallas_call(
        pair_up,
        in_specs=[VMEM] * 3,
        out_specs=VMEM,
        out_shape=jax.ShapeDtypeStruct((32, SLOT, HD), jnp.bfloat16),
        compiler_params=pltpu.CompilerParams(vmem_limit_bytes=24 * MIB),
        cost_estimate=pl.CostEstimate(flops=4_000_000, bytes_accessed=2_000_000, transcendentals=1000),
    )(peer, own, own_st)


def merge(msg_ref, out_ref):
    msg = msg_ref[...].astype(jnp.float32)
    top, total, dot = spread_stats(msg[:, 48:56])
    factor = jnp.exp2((top - jnp.max(top, axis=0, keepdims=True)) * SCALE2)
    total = factor * total
    whole = jnp.sum(total, axis=0, keepdims=True)
    lag = factor * (dot - jnp.sum(total * dot, axis=0, keepdims=True) / whole)
    scale = (SCALE / whole)[0]
    rows = []
    for part in range(PARTS):
        at = part * 16
        grad = jnp.sum(
            column(factor, part) * msg[:, at : at + 8] + column(lag, part) * msg[:, at + 8 : at + 16], axis=0
        )
        rows.append(grad * column(scale, part))
    block = jnp.concatenate(rows, axis=0).astype(jnp.bfloat16)
    out_ref[...] = jnp.broadcast_to(block[None], out_ref.shape)


def merge_call(msg):
    return pl.pallas_call(
        merge,
        in_specs=[VMEM],
        out_specs=VMEM,
        out_shape=jax.ShapeDtypeStruct((32, 8 * PARTS, HD), jnp.bfloat16),
        compiler_params=pltpu.CompilerParams(vmem_limit_bytes=16 * MIB),
        cost_estimate=pl.CostEstimate(flops=4_000_000, bytes_accessed=800_000, transcendentals=1000),
    )(msg)


def squares_of(msg_ref, out_ref):
    grad = msg_ref[...].astype(jnp.float32)
    total = jnp.sum(jnp.sum(grad * grad, axis=0), axis=0, keepdims=True)
    out_ref[...] = jnp.broadcast_to(jnp.sum(total, axis=1, keepdims=True)[None], out_ref.shape)


def squares_call(msg):
    return pl.pallas_call(
        squares_of,
        in_specs=[VMEM],
        out_specs=VMEM,
        out_shape=jax.ShapeDtypeStruct((8, 8, HD), jnp.float32),
        compiler_params=pltpu.CompilerParams(vmem_limit_bytes=16 * MIB),
        cost_estimate=pl.CostEstimate(flops=200_000, bytes_accessed=230_000, transcendentals=0),
    )(msg)


def finish(own_ref, peer_ref, sum_ref, out_ref):
    core = lax.axis_index("c")
    squares = jnp.sum(sum_ref[...], axis=0)[:1]
    factor = 1.0 / jnp.sqrt(squares / (B * QT * HQ * HD) + EPSILON)
    for ref, odd in ((own_ref, core), (peer_ref, 1 - core)):
        rows = ref[...].astype(jnp.float32) * factor
        for part in range(PARTS):
            out_ref[2 * part + odd] = rows[:, part * 8 : part * 8 + 8].reshape(QT, 32, HD).astype(jnp.bfloat16)


def finish_call(own, peer, sums):
    return pl.pallas_call(
        finish,
        in_specs=[VMEM] * 3,
        out_specs=VMEM,
        out_shape=jax.ShapeDtypeStruct((B, QT, 32, HD), jnp.bfloat16),
        compiler_params=pltpu.CompilerParams(vmem_limit_bytes=16 * MIB),
        cost_estimate=pl.CostEstimate(flops=200_000, bytes_accessed=800_000, transcendentals=0),
    )(own, peer, sums)


def local(queries, key_cache, value_cache, grad_out, cache_len):
    swap = [(0, 1), (1, 0)]
    with jax.named_scope("attend"):
        peer, own, own_st = attend_call(cache_len, queries, key_cache, value_cache, grad_out)
    with jax.named_scope("pair"):
        peer = lax.ppermute(peer, "c", swap)
        msg = pair_up_call(peer, own, own_st)
    with jax.named_scope("exchange"):
        msg = lax.all_to_all(msg, ("z", "y"), 0, 0)
    with jax.named_scope("merge"):
        msg = merge_call(msg)
    with jax.named_scope("spread"):
        msg = lax.all_to_all(msg, ("z", "y"), 0, 0)
    with jax.named_scope("norm"):
        other = lax.ppermute(msg, "c", swap)
        sums = lax.all_to_all(squares_call(msg), ("c", "x"), 0, 0)
        return finish_call(msg, other, sums)


def solution(mesh):
    fine = Mesh(mesh.devices.reshape(8, 4, 2, 4), ("z", "y", "c", "x"))
    seq = ("z", "y", "c")
    placed = (
        P(None, None, "x", None),
        P(None, seq, "x", None),
        P(None, seq, "x", None),
        P(None, None, "x", None),
        P(),
    )
    return jax.shard_map(
        local, mesh=fine, in_specs=placed, out_specs=P(None, None, "x", None), check_vma=False
    )
```

```python
import math

import jax
import jax.numpy as jnp
from jax import lax
from jax.experimental import pallas as pl
from jax.experimental.pallas import tpu as pltpu
from jax.sharding import Mesh
from jax.sharding import PartitionSpec as P

B = 6
QT = 8
HQ = 128
HD = 128

NEGATIVE = -1e30
FLOOR = -1e29
EPSILON = 1e-06
SCALE = 1.0 / math.sqrt(HD)
SCALE2 = SCALE * math.log2(math.e)
CHUNK = 256
SPLIT = 512
PARTS = 3
SLOT = 56
MIB = 1024 * 1024
VMEM = pl.BlockSpec(memory_space=pltpu.VMEM)
HBM = pl.BlockSpec(memory_space=pltpu.HBM)
FIRST = (((0,), (0,)), ((), ()))


def high(x):
    return x.astype(jnp.bfloat16).astype(jnp.float32)


def attend(
    len_ref, q_hbm, k_hbm, v_hbm, go_hbm, peer_ref, own_ref, own_st_ref,
    q_buf, go_buf, k_buf, v_buf, s_a, s_b, s_c, g_a, g_b, g_c,
    d_a, d_b, d_c, sems,
):
    core = lax.axis_index("c")
    count, rows = k_buf.shape[0], k_buf.shape[1]
    span = rows // 2
    chunks = -(-span // CHUNK)
    start = ((lax.axis_index("z") * 4 + lax.axis_index("y")) * 2 + core) * span

    def sequence(j):
        return 2 * j + 1 - core if j < PARTS else 2 * (j - PARTS) + core

    def place(i):
        first = i * CHUNK
        return first, min(CHUNK, span - first)

    def whole(source, target, base):
        return [
            pltpu.make_async_copy(source.at[sequence(j)], target.at[j], sems.at[base + j]) for j in range(count)
        ]

    def first_part(source, target, half, sem):
        begin, end = (0, SPLIT) if half == 0 else (SPLIT, span)
        at = pl.ds(2 * begin, 2 * (end - begin))
        return pltpu.make_async_copy(source.at[sequence(0), at], target.at[0, at], sems.at[sem])

    keys, values = whole(k_hbm, k_buf, 0), whole(v_hbm, v_buf, count)
    small = list(zip(whole(q_hbm, q_buf, 2 * count), whole(go_hbm, go_buf, 3 * count)))
    early = [first_part(k_hbm, k_buf, 0, 0), first_part(v_hbm, v_buf, 0, count)]
    late = [first_part(k_hbm, k_buf, 1, 4 * count), first_part(v_hbm, v_buf, 1, 4 * count + 1)]
    for copy in (*small[0], *early, *late):
        copy.start()
    for j in range(1, count):
        for copy in (small[j][0], keys[j], small[j][1], values[j]):
            copy.start()

    scores, probs, splits = (s_a, s_b, s_c), (g_a, g_b, g_c), (d_a, d_b, d_c)
    lead = lax.broadcasted_iota(jnp.int32, (8, 128), 1) // 16 - lax.broadcasted_iota(jnp.int32, (8, 128), 0)

    def turned(x):
        blank = jnp.zeros((HD, 128), jnp.bfloat16)
        left = jnp.concatenate([x[:, :16].reshape(128, HD).T, blank], axis=0)
        right = jnp.concatenate([blank, x[:, 16:].reshape(128, HD).T], axis=0)
        return jnp.concatenate([left, right], axis=1)

    def sides(x, reduce):
        return reduce(x, axis=0, keepdims=True)

    def split(source, j, i):
        first, size = place(i)
        return source[j, 2 * first : 2 * (first + size), :].reshape(size, 2 * HD)

    def score_step(j, i, qt, gt, room, top):
        first, size = place(i)
        at = slice(first, first + size)
        kd = split(k_buf, j, i)
        splits[j % 3][at, :] = kd
        s = jnp.dot(kd, qt, preferred_element_type=jnp.float32)
        tile_start = lax.broadcasted_iota(jnp.int32, (size // 8, 8, 128), 0) * 8
        visible = (room + lead - first)[None] >= tile_start
        peaks = []
        for side in range(2):
            cols = slice(side * 128, side * 128 + 128)
            half = jnp.where(visible, s[:, cols].reshape(size // 8, 8, 128), NEGATIVE)
            scores[j % 3][at, cols] = half.reshape(size, 128)
            peaks.append(jnp.max(half, axis=0))
        vd = split(v_buf, j, i)
        probs[j % 3][at, :] = jnp.dot(vd, gt, preferred_element_type=jnp.float32)
        return jnp.maximum(top, jnp.concatenate(peaks, axis=1))

    def weight_step(j, i, tops, total, dot):
        first, size = place(i)
        at = slice(first, first + size)
        s = scores[j % 3][at, :].reshape(size // 8, 8, 256)
        w = jnp.exp2((s - tops[None]) * SCALE2)
        scores[j % 3][at, :] = w.reshape(size, 256)
        wg = w * probs[j % 3][at, :].reshape(size // 8, 8, 256)
        return total + jnp.sum(w, axis=0), dot + jnp.sum(wg, axis=0)

    def term_step(j, i, dots, acc):
        first, size = place(i)
        at = slice(first, first + size)
        w = scores[j % 3][at, :]
        p = w * (probs[j % 3][at, :] - dots)
        out = []
        for side in range(2):
            cols = slice(side * 128, side * 128 + 128)
            pw = jnp.concatenate([p[:, cols], w[:, cols]], axis=1).astype(jnp.bfloat16)
            out.append(
                acc[side]
                + lax.dot_general(splits[j % 3][at, cols], pw, FIRST, preferred_element_type=jnp.float32)
            )
        return out

    def prepare(j):
        seq = sequence(j)
        for copy in (*small[j], *(early if j == 0 else (keys[j], values[j]))):
            copy.wait()
        return turned(q_buf[j]), turned(go_buf[j]), len_ref[seq] - QT - start

    def means_of(total, dot):
        total, dot = sides(total, jnp.sum), sides(dot, jnp.sum)
        return total, jnp.where(total > 0.0, dot / jnp.where(total > 0.0, total, 1.0), 0.0)

    def store(j, acc, tops, totals, dots):
        pieces = []
        for half in (slice(0, 128), slice(128, 256)):
            pair = [acc[side][:, half].T.reshape(8, 16, 128) for side in range(2)]
            pieces.append(jnp.concatenate(pair, axis=1).reshape(32, 8, 128))
        both = jnp.concatenate(pieces, axis=1)
        part = j % PARTS
        if j < PARTS:
            peer_ref[:, part * 16 : part * 16 + 16, :] = both.astype(jnp.bfloat16)
        else:
            own_ref[:, part * 16 : part * 16 + 16, :] = both
        sub = lax.broadcasted_iota(jnp.int32, (8, 128), 0)
        for side in range(2):
            at = slice(side * 128, side * 128 + 128)
            m, t, d = tops[:, at], totals[:, at], dots[:, at]
            cols = (m, high(t), t - high(t), high(d), d - high(d)) if j < PARTS else (m, t, d)
            block = jnp.zeros((8, 128), jnp.float32)
            for k, col in enumerate(cols):
                block = jnp.where(sub == k, col, block)
            blocks[j // PARTS, side, part] = block

    blocks = {}
    zero8 = jnp.zeros((8, 256), jnp.float32)
    stats = {}
    for n in range(count + 2):
        first, second, third = n, n - 1, n - 2
        if first < count:
            ready = prepare(first)
            top = jnp.full((8, 256), NEGATIVE, jnp.float32)
        if 0 <= second < count:
            tops = high(jnp.maximum(sides(last_top, jnp.max), FLOOR))
            total, dot = zero8, zero8
        if 0 <= third:
            acc = [jnp.zeros((128, 256), jnp.float32)] * 2
        for i in range(chunks):
            if first == 0 and i * CHUNK == SPLIT:
                for copy in late:
                    copy.wait()
            if 0 <= third:
                acc = term_step(third, i, stats[third][2], acc)
            if first < count:
                top = score_step(first, i, *ready, top)
            if 0 <= second < count:
                total, dot = weight_step(second, i, tops, total, dot)
        if 0 <= third:
            store(third, acc, *stats[third])
        if 0 <= second < count:
            stats[second] = (tops, *means_of(total, dot))
        last_top = top

    blank = jnp.zeros((8, 128), jnp.float32)
    z = jnp.concatenate(
        [blocks.get((who, side, part), blank) for who in range(2) for side in range(2) for part in range(4)], axis=0
    ).T
    for who in range(2):
        pair = []
        for side in range(2):
            shift = (128 - who * 64 - side * 32) % 128
            pair.append((pltpu.roll(z, shift, 1) if shift else z).reshape(8, 16, 128))
        st = jnp.concatenate(pair, axis=1).reshape(32, 8, 128)
        if who == 0:
            peer_ref[:, 48:64, :] = jnp.concatenate([st, jnp.zeros_like(st)], axis=1).astype(jnp.bfloat16)
        else:
            own_st_ref[...] = st


def attend_call(lengths, q, k, v, go):
    count, span = k.shape[0], k.shape[1]
    q, k, v, go = (
        pltpu.with_memory_space_constraint(x, pltpu.HBM)
        for x in (q, k.reshape(count, span * 2, HD), v.reshape(count, span * 2, HD), go)
    )
    wide = pltpu.VMEM((span, 256), jnp.float32)
    slim = pltpu.VMEM((span, 256), jnp.bfloat16)
    return pl.pallas_call(
        attend,
        in_specs=[pl.BlockSpec(memory_space=pltpu.SMEM), HBM, HBM, HBM, HBM],
        out_specs=[VMEM, VMEM, VMEM],
        out_shape=[
            pltpu.VMEM((32, 64, HD), jnp.bfloat16),
            pltpu.VMEM((32, 48, HD), jnp.float32),
            pltpu.VMEM((32, 8, HD), jnp.float32),
        ],
        scratch_shapes=[
            pltpu.VMEM(q.shape, jnp.bfloat16),
            pltpu.VMEM(go.shape, jnp.bfloat16),
            pltpu.VMEM(k.shape, jnp.bfloat16),
            pltpu.VMEM(v.shape, jnp.bfloat16),
            wide, wide, wide, wide, wide, wide, slim, slim, slim,
            pltpu.SemaphoreType.DMA((4 * count + 2,)),
        ],
        compiler_params=pltpu.CompilerParams(vmem_limit_bytes=56 * MIB),
        cost_estimate=pl.CostEstimate(flops=4_500_000_000, bytes_accessed=14_000_000, transcendentals=3_000_000),
    )(lengths, q, k, v, go)


def shifted(st, k):
    return pltpu.roll(st.reshape(256, 128), 128 - k, 1).reshape(32, 8, 128)


def spread_stats(st):
    return st, shifted(st, 1) + shifted(st, 2), shifted(st, 3) + shifted(st, 4)


def column(x, part):
    return x[..., 8 * part : 8 * part + 1]


def pair_up(peer_ref, own_ref, own_st_ref, out_ref):
    peer = peer_ref[...].astype(jnp.float32)
    own = own_ref[...]
    own_st = own_st_ref[...]
    top_a, total_a, dot_a = own_st, shifted(own_st, 1), shifted(own_st, 2)
    top_b, total_b, dot_b = spread_stats(peer[:, 48:56])
    top = jnp.maximum(top_a, top_b)
    factor_a = jnp.exp2((top_a - top) * SCALE2)
    factor_b = jnp.exp2((top_b - top) * SCALE2)
    total_a, total_b = factor_a * total_a, factor_b * total_b
    total = total_a + total_b
    dot = (total_a * dot_a + total_b * dot_b) / jnp.where(total > 0.0, total, 1.0)
    lag_a, lag_b = factor_a * (dot_a - dot), factor_b * (dot_b - dot)
    pieces = []
    for part in range(PARTS):
        at = part * 16
        term_a, term_b = own[:, at : at + 8], peer[:, at : at + 8]
        mass_a, mass_b = own[:, at + 8 : at + 16], peer[:, at + 8 : at + 16]
        take_a, take_b = column(factor_a, part), column(factor_b, part)
        pieces.append(
            take_a * term_a + column(lag_a, part) * mass_a + (take_b * term_b + column(lag_b, part) * mass_b)
        )
        pieces.append(take_a * mass_a + take_b * mass_b)
    lane = lax.broadcasted_iota(jnp.int32, (32, 8, 128), 2)
    st = jnp.zeros((32, 8, 128), jnp.float32)
    for k, value in enumerate((top, high(total), total - high(total), high(dot), dot - high(dot))):
        st = jnp.where((lane % 8 == k) & (lane < 8 * PARTS), shifted(value, 128 - k) if k else value, st)
    out_ref[...] = jnp.concatenate(pieces + [st], axis=1).astype(jnp.bfloat16)


def pair_up_call(peer, own, own_st):
    return pl.pallas_call(
        pair_up,
        in_specs=[VMEM] * 3,
        out_specs=VMEM,
        out_shape=jax.ShapeDtypeStruct((32, SLOT, HD), jnp.bfloat16),
        compiler_params=pltpu.CompilerParams(vmem_limit_bytes=24 * MIB),
        cost_estimate=pl.CostEstimate(flops=4_000_000, bytes_accessed=2_000_000, transcendentals=1000),
    )(peer, own, own_st)


def merge(msg_ref, out_ref):
    msg = msg_ref[...].astype(jnp.float32)
    top, total, dot = spread_stats(msg[:, 48:56])
    factor = jnp.exp2((top - jnp.max(top, axis=0, keepdims=True)) * SCALE2)
    total = factor * total
    whole = jnp.sum(total, axis=0, keepdims=True)
    lag = factor * (dot - jnp.sum(total * dot, axis=0, keepdims=True) / whole)
    scale = (SCALE / whole)[0]
    rows = []
    for part in range(PARTS):
        at = part * 16
        grad = jnp.sum(
            column(factor, part) * msg[:, at : at + 8] + column(lag, part) * msg[:, at + 8 : at + 16], axis=0
        )
        rows.append(grad * column(scale, part))
    block = jnp.concatenate(rows, axis=0).astype(jnp.bfloat16)
    out_ref[...] = jnp.broadcast_to(block[None], out_ref.shape)


def merge_call(msg):
    return pl.pallas_call(
        merge,
        in_specs=[VMEM],
        out_specs=VMEM,
        out_shape=jax.ShapeDtypeStruct((32, 8 * PARTS, HD), jnp.bfloat16),
        compiler_params=pltpu.CompilerParams(vmem_limit_bytes=16 * MIB),
        cost_estimate=pl.CostEstimate(flops=4_000_000, bytes_accessed=800_000, transcendentals=1000),
    )(msg)


def squares_of(msg_ref, out_ref):
    grad = msg_ref[...].astype(jnp.float32)
    total = jnp.sum(jnp.sum(grad * grad, axis=0), axis=0, keepdims=True)
    out_ref[...] = jnp.broadcast_to(jnp.sum(total, axis=1, keepdims=True)[None], out_ref.shape)


def squares_call(msg):
    return pl.pallas_call(
        squares_of,
        in_specs=[VMEM],
        out_specs=VMEM,
        out_shape=jax.ShapeDtypeStruct((8, 8, HD), jnp.float32),
        compiler_params=pltpu.CompilerParams(vmem_limit_bytes=16 * MIB),
        cost_estimate=pl.CostEstimate(flops=200_000, bytes_accessed=230_000, transcendentals=0),
    )(msg)


def finish(own_ref, peer_ref, sum_ref, out_hbm, rows_buf, sems):
    core = lax.axis_index("c")
    squares = jnp.sum(sum_ref[...], axis=0)[:1]
    factor = 1.0 / jnp.sqrt(squares / (B * QT * HQ * HD) + EPSILON)
    copies = []
    for ref, odd in ((own_ref, core), (peer_ref, 1 - core)):
        rows = ref[...].astype(jnp.float32) * factor
        for part in range(PARTS):
            slot = len(copies)
            rows_buf[slot] = rows[:, part * 8 : part * 8 + 8].reshape(QT, 32, HD).astype(jnp.bfloat16)
            copies.append(pltpu.make_async_copy(rows_buf.at[slot], out_hbm.at[2 * part + odd], sems.at[slot]))
            copies[slot].start()
    for copy in copies:
        copy.wait()


def finish_call(own, peer, sums):
    return pl.pallas_call(
        finish,
        in_specs=[VMEM] * 3,
        out_specs=HBM,
        out_shape=jax.ShapeDtypeStruct((B, QT, 32, HD), jnp.bfloat16),
        scratch_shapes=[pltpu.VMEM((B, QT, 32, HD), jnp.bfloat16), pltpu.SemaphoreType.DMA((B,))],
        compiler_params=pltpu.CompilerParams(vmem_limit_bytes=16 * MIB),
        cost_estimate=pl.CostEstimate(flops=200_000, bytes_accessed=800_000, transcendentals=0),
    )(own, peer, sums)


def local(queries, key_cache, value_cache, grad_out, cache_len):
    swap = [(0, 1), (1, 0)]
    with jax.named_scope("attend"):
        peer, own, own_st = attend_call(cache_len, queries, key_cache, value_cache, grad_out)
    with jax.named_scope("pair"):
        peer = lax.ppermute(peer, "c", swap)
        msg = pair_up_call(peer, own, own_st)
    with jax.named_scope("exchange"):
        msg = lax.all_to_all(msg, ("z", "y"), 0, 0)
    with jax.named_scope("merge"):
        msg = merge_call(msg)
    with jax.named_scope("spread"):
        msg = lax.all_to_all(msg, ("z", "y"), 0, 0)
    with jax.named_scope("norm"):
        other = lax.ppermute(msg, "c", swap)
        sums = lax.all_to_all(squares_call(msg), ("c", "x"), 0, 0)
        return finish_call(msg, other, sums)


def solution(mesh):
    fine = Mesh(mesh.devices.reshape(8, 4, 2, 4), ("z", "y", "c", "x"))
    seq = ("z", "y", "c")
    placed = (
        P(None, None, "x", None),
        P(None, seq, "x", None),
        P(None, seq, "x", None),
        P(None, None, "x", None),
        P(),
    )
    return jax.shard_map(
        local, mesh=fine, in_specs=placed, out_specs=P(None, None, "x", None), check_vma=False
    )
```
